256 devices in a mesh: dp: 16 (over z, core), tensor: 16 (over x, y).
Axes of the slice: x: 4, y: 4, z: 8, core: 2. Of those that a mesh axis runs over, the one named last changes fastest.
Arguments:
- acts: bfloat16 [32768, 8192], P('dp', 'tensor'), may hold values from -6 to 6
- grads: bfloat16 [32768, 28672], P('dp', 'tensor'), may hold values from -6 to 6
- sketch: float32 [64, 28672], P(None, 'tensor'), may hold values from -6 to 6
- picks: int32 [32768], P('dp'), may hold values from 0 to 2047
Outputs:
- adapter_down_weight: float32 [64, 28672], P(None, 'tensor')
- adapter_up_weight: float32 [64, 8192], P(None, 'tensor')
The draws below stay inside these ranges and needn't reach their ends.
Inputs may be any that keep to these rules, and one draw needn't show every extreme that they name: picks[t] is a row of the 2048 rows of token t's own block of the pool, the block of rows (t // 2048) * 2048 onwards.
All inputs are finite; a program needn't handle non-finite values.
Results may differ from the reference program's by a relative error of at most 0.0003.
Values sent between devices are 32-bit elements; how exact they have to be, the bound alone decides.
No kernel may reach another device: no remote copies, remote signals or barrier semaphores. Data moves between devices by JAX's collectives and lax.ppermute only.
A program may use at most 128 MiB of HBM per device.

```python
import math
import jax
import jax.numpy as jnp
from jax import lax

MODEL_WIDTH = 8192
F = 28672
R = 64
ITERS = 2
TOK_DEV = 2048
SAMPLED_TOKENS = 32768
N_DP = 16


def with_ends(drawn, rng, least, top_value):
    extent = drawn.shape
    index_at = [jax.random.randint(jax.random.fold_in(rng, axis), (), 0, extent[axis]) for axis in range(len(extent))]
    drawn = drawn.at[tuple(index_at)].set(least)
    longest = extent.index(max(extent))
    index_at[longest] = (index_at[longest] + 1) % extent[longest]
    return drawn.at[tuple(index_at)].set(top_value)


def levels(key, shape, shards, smallest, top_value):
    factor_of = 1.0
    for position, shards_of in shards:
        draws = jax.random.uniform(jax.random.fold_in(jax.random.fold_in(key, 6), position), (shards_of,), jnp.float32, smallest / len(shards), top_value / len(shards))
        factor_of = factor_of * jnp.repeat(jnp.exp(draws), shape[position] // shards_of).reshape((-1,) + (1,) * (len(shape) - 1 - position))
    return factor_of


def normal_values(own_key, extent, scale, most, cuts=(), kind=jnp.bfloat16):
    entries = jax.random.normal(own_key, extent, jnp.float32) * scale
    if len(cuts) > 0:
        entries = levels(own_key, extent, cuts, -0.22, 0.18) * entries
    return jnp.clip(entries, min=-most, max=most).astype(kind)


def setup_inputs(seed: int = 0) -> dict:
    streams_of = jax.random.split(jax.random.key(seed), 5)
    acts = normal_values(streams_of[0], (SAMPLED_TOKENS, MODEL_WIDTH), 1.0, 6.0, ((0, 16), (1, 16)))
    grads = normal_values(streams_of[1], (SAMPLED_TOKENS, F), 1.0, 6.0, ((0, 16), (1, 16)))
    sketch = normal_values(streams_of[2], (R, F), 1.0, 6.0, ((1, 16),), jnp.float32)
    picks = with_ends(jax.random.randint(streams_of[3], (SAMPLED_TOKENS,), 0, TOK_DEV), jax.random.fold_in(streams_of[3], 1), 0, TOK_DEV - 1).astype(jnp.int32)
    return {"acts": acts, "grads": grads, "sketch": sketch, "picks": picks}


def orthonormal(rows_t):
    gram = jnp.dot(rows_t.astype(jnp.float32), rows_t.T.astype(jnp.float32), precision=lax.Precision.HIGHEST, preferred_element_type=jnp.float32)
    factor_low = jnp.linalg.cholesky(gram)
    return lax.linalg.triangular_solve(factor_low, rows_t, left_side=True, lower=True)

def reference(acts, grads, sketch, picks):
    high = lax.Precision.HIGHEST
    acts_blocks = acts.reshape(N_DP, TOK_DEV, MODEL_WIDTH)
    grad_blocks = grads.reshape(N_DP, TOK_DEV, F)
    pick_blocks = picks.reshape(N_DP, TOK_DEV).astype(jnp.int32)

    def apply_grad(left_t):

        def visit(carry, inputs):
            block_x, block_g, block_p = inputs
            sample_x = jnp.take(block_x, block_p, axis=0).astype(jnp.float32)
            sampled_gradient = jnp.take(block_g, block_p, axis=0).astype(jnp.float32)
            proj = jnp.dot(left_t.astype(jnp.float32), sampled_gradient.T.astype(jnp.float32), precision=high, preferred_element_type=jnp.float32)
            return (carry + jnp.dot(proj.astype(jnp.float32), sample_x.astype(jnp.float32), precision=high, preferred_element_type=jnp.float32), None)
        total, _ = lax.scan(visit, jnp.zeros((R, MODEL_WIDTH), jnp.float32), (acts_blocks, grad_blocks, pick_blocks))
        return total

    def transpose_product(basis_transposed):

        def visit(carry, inputs):
            block_x, block_g, block_p = inputs
            sample_x = jnp.take(block_x, block_p, axis=0).astype(jnp.float32)
            sampled_gradient = jnp.take(block_g, block_p, axis=0).astype(jnp.float32)
            proj = jnp.dot(basis_transposed.astype(jnp.float32), sample_x.T.astype(jnp.float32), precision=high, preferred_element_type=jnp.float32)
            return (carry + jnp.dot(proj.astype(jnp.float32), sampled_gradient.astype(jnp.float32), precision=high, preferred_element_type=jnp.float32), None)
        total, _ = lax.scan(visit, jnp.zeros((R, F), jnp.float32), (acts_blocks, grad_blocks, pick_blocks))
        return total
    subspace_basis = orthonormal(apply_grad(sketch))
    for step in range(ITERS):
        right = orthonormal(transpose_product(subspace_basis))
        subspace_basis = orthonormal(apply_grad(right))
    adapter_down_weight = transpose_product(subspace_basis) / math.sqrt(SAMPLED_TOKENS)
    adapter_up_weight = subspace_basis * math.sqrt(MODEL_WIDTH)
    return (adapter_down_weight, adapter_up_weight)
```

```python
import math

import jax
import jax.numpy as jnp
from jax import lax
from jax.sharding import PartitionSpec as P

MODEL_WIDTH = 8192
ITERS = 2
R = 64
HIGH = lax.Precision.HIGHEST


def pieces(m):
    hi = lax.reduce_precision(m, 8, 7)
    rest = m - hi
    mid = lax.reduce_precision(rest, 8, 7)
    low = rest - mid
    return jnp.concatenate([hi, mid, low], axis=0).astype(jnp.bfloat16)


def whole(out):
    return out[:R] + (out[R : 2 * R] + out[2 * R :])


def times_transposed(m, w):
    return whole(
        lax.dot_general(
            pieces(m), w, (((1,), (1,)), ((), ())), preferred_element_type=jnp.float32
        )
    )


def times(m, w):
    return whole(jnp.dot(pieces(m), w, preferred_element_type=jnp.float32))


def counts_of(picks):
    tok = picks.shape[0]
    high_at = (picks[None, :] // 128 == jnp.arange(tok // 128, dtype=jnp.int32)[:, None])
    low_at = (picks[:, None] % 128 == jnp.arange(128, dtype=jnp.int32)[None, :])
    found = jnp.dot(
        high_at.astype(jnp.bfloat16),
        low_at.astype(jnp.bfloat16),
        preferred_element_type=jnp.float32,
    )
    return found.reshape(1, tok)


def tensor_sum(part):
    n = part.shape[0]
    mine = jnp.sum(lax.all_to_all(part, "tensor", 0, 0), axis=0)
    return lax.all_to_all(jnp.broadcast_to(mine[None], (n,) + mine.shape), "tensor", 0, 0)


def token_totals(m, w, with_gram):
    prod = times_transposed(m, w)
    n = prod.shape[1] // 128
    part = prod.reshape(R, n, 128).transpose(1, 0, 2)
    if with_gram:
        gram = jnp.dot(m, m.T, precision=HIGH, preferred_element_type=jnp.float32)
        gram = gram.reshape(n, R // n, R)
        gram = jnp.pad(gram, ((0, 0), (0, 8 - R // n), (0, 128 - R)))
        part = jnp.concatenate([part, gram], axis=1)
    total = tensor_sum(part)
    prod = total[:, :R].transpose(1, 0, 2).reshape(R, n * 128)
    if not with_gram:
        return prod, None
    return prod, total[:, R : R + R // n, :R].reshape(R, R)


def inverse_factor(gram):
    factor = jnp.linalg.cholesky(gram)
    eye = jnp.eye(R, dtype=jnp.float32)
    return lax.linalg.triangular_solve(factor, eye, left_side=True, lower=True)


def apply_left(factor, m):
    return jnp.dot(factor, m, precision=HIGH, preferred_element_type=jnp.float32)


def feature_totals(part):
    n = part.shape[1]
    size = lax.axis_size("dp")
    nz = size // 2
    swap = [(i, i ^ 1) for i in range(size)]
    groups = [[2 * z + c for z in range(nz)] for c in range(2)]
    core = lax.axis_index("dp") % 2
    blocks = part.reshape(2, R // 16, 8, 2, n // 2).transpose(0, 1, 3, 2, 4)
    blocks = blocks.reshape(2, nz, 8, n // 2)
    kept = lax.dynamic_index_in_dim(blocks, core, 0, keepdims=False)
    sent = lax.dynamic_index_in_dim(blocks, 1 - core, 0, keepdims=False)
    half = kept + lax.ppermute(sent, "dp", swap)
    own = jnp.sum(lax.all_to_all(half, "dp", 0, 0, axis_index_groups=groups), axis=0)
    half = lax.all_to_all(
        jnp.broadcast_to(own[None], (nz,) + own.shape), "dp", 0, 0, axis_index_groups=groups
    )
    other = lax.ppermute(half, "dp", swap)
    full = jnp.where(core == 0, jnp.stack([half, other]), jnp.stack([other, half]))
    return full.reshape(2, R // 16, 2, 8, n // 2).transpose(0, 1, 3, 2, 4).reshape(R, n)


def per_device(acts, grads, sketch, picks):
    token_count_overall = picks.shape[0] * lax.axis_size("dp")
    counts = counts_of(picks)
    proj, _ = token_totals(sketch, grads, False)
    range_t = feature_totals(times(proj * counts, acts))
    for step in range(ITERS):
        proj, gram = token_totals(range_t, acts, True)
        proj = apply_left(inverse_factor(gram), proj)
        co_range = feature_totals(times(proj * counts, grads))
        proj, gram = token_totals(co_range, grads, True)
        proj = apply_left(inverse_factor(gram), proj)
        range_t = feature_totals(times(proj * counts, acts))
    proj, gram = token_totals(range_t, acts, True)
    factor = inverse_factor(gram)
    proj = apply_left(factor, proj)
    adapter_down_weight = feature_totals(times(proj * counts, grads)) / math.sqrt(
        token_count_overall
    )
    adapter_up_weight = apply_left(factor, range_t) * math.sqrt(MODEL_WIDTH)
    return (adapter_down_weight, adapter_up_weight)


def solution(mesh):
    return jax.shard_map(
        per_device,
        mesh=mesh,
        in_specs=(P("dp", "tensor"), P("dp", "tensor"), P(None, "tensor"), P("dp")),
        out_specs=(P(None, "tensor"), P(None, "tensor")),
        check_vma=False,
    )
```

```python
import math

import jax
import jax.numpy as jnp
from jax import lax
from jax.experimental import pallas as pl
from jax.experimental.pallas import tpu as pltpu
from jax.sharding import PartitionSpec as P

MODEL_WIDTH = 8192
ITERS = 2
R = 64
HIGH = lax.Precision.HIGHEST


def pieces(m):
    hi = lax.reduce_precision(m, 8, 7)
    rest = m - hi
    mid = lax.reduce_precision(rest, 8, 7)
    low = rest - mid
    return jnp.concatenate([hi, mid, low], axis=0).astype(jnp.bfloat16)


def whole(out):
    return out[:R] + (out[R : 2 * R] + out[2 * R :])


def times_transposed(stack, w):
    return whole(
        lax.dot_general(stack, w, (((1,), (1,)), ((), ())), preferred_element_type=jnp.float32)
    )


def times(m, w):
    return whole(jnp.dot(pieces(m), w, preferred_element_type=jnp.float32))


def gram_of(stack):
    g = lax.dot_general(
        stack, stack, (((1,), (1,)), ((), ())), preferred_element_type=jnp.float32
    )
    part = [[g[R * i : R * i + R, R * j : R * j + R] for j in range(3)] for i in range(3)]
    small = (part[1][2] + part[2][1]) + part[2][2]
    middle = (part[0][2] + part[2][0]) + part[1][1]
    return part[0][0] + ((part[0][1] + part[1][0]) + (middle + small))


def added(blocks):
    terms = [blocks[i] for i in range(blocks.shape[0])]
    while len(terms) > 1:
        terms = [terms[i] + terms[i + 1] for i in range(0, len(terms), 2)]
    return terms[0]


def counts_of(picks):
    tok = picks.shape[0]
    high_at = (picks[None, :] // 128 == jnp.arange(tok // 128, dtype=jnp.int32)[:, None])
    low_at = (picks[:, None] % 128 == jnp.arange(128, dtype=jnp.int32)[None, :])
    found = jnp.dot(
        high_at.astype(jnp.bfloat16),
        low_at.astype(jnp.bfloat16),
        preferred_element_type=jnp.float32,
    )
    return found.reshape(1, tok)


def token_totals(m, w, with_gram):
    stack = pieces(m)
    prod = times_transposed(stack, w)
    n = prod.shape[1] // 128
    part = prod.reshape(R, n, 128).transpose(1, 0, 2)
    if with_gram:
        gram = gram_of(stack).reshape(n, R // n, R)
        gram = jnp.pad(gram, ((0, 0), (0, 8 - R // n), (0, 128 - R)))
        part = jnp.concatenate([part, gram], axis=1)
    mine = added(lax.all_to_all(part, "tensor", 0, 0))
    total = lax.all_to_all(jnp.broadcast_to(mine[None], part.shape), "tensor", 0, 0)
    prod = total[:, :R].transpose(1, 0, 2).reshape(R, n * 128)
    if not with_gram:
        return prod, None
    return prod, inverse_factor(total[:, R : R + R // n, :R].reshape(R, R))


def inverse_factor_kernel(gram_ref, out_ref):
    shape = (8, 2 * R)
    lanes = lax.broadcasted_iota(jnp.int32, shape, 1)
    sub = lax.broadcasted_iota(jnp.int32, shape, 0)
    n = R // 8
    tiles = []
    for i in range(n):
        tile = jnp.concatenate(
            [gram_ref[8 * i : 8 * i + 8, :], jnp.zeros((8, R), jnp.float32)], axis=1
        )
        tiles.append(jnp.where(lanes == sub + (R + 8 * i), 1.0, tile))

    def column(x, j):
        return jnp.broadcast_to(x[:, j : j + 1], shape)

    def row(x, j):
        return jnp.broadcast_to(x[j : j + 1, :], shape)

    for t in range(n):
        block = tiles[t]
        cols = [column(block, 8 * t + k) for k in range(8)]
        below = [[column(tiles[i], 8 * t + k) for k in range(8)] for i in range(t + 1, n)]
        out = block
        for s in range(8):
            here = sub == s
            pivot = row(cols[s], s)
            inv = 1.0 / pivot
            factor = cols[s] * inv
            for k in range(s + 1, 8):
                across = row(cols[k], s)
                cols[k] = jnp.where(here, across * inv, cols[k] - factor * across)
            across = row(block, s)
            out = jnp.where(here, across * lax.rsqrt(pivot), out)
            block = jnp.where(here, across * inv, block - factor * across)
        out_ref[8 * t : 8 * t + 8, :] = out[:, R:]
        rows = [row(block, k) for k in range(8)]
        for i in range(t + 1, n):
            terms = [c * r for c, r in zip(below[i - t - 1], rows)]
            while len(terms) > 1:
                terms = [terms[k] + terms[k + 1] for k in range(0, len(terms), 2)]
            tiles[i] = tiles[i] - terms[0]


def inverse_factor(gram):
    return pl.pallas_call(
        inverse_factor_kernel,
        out_shape=jax.ShapeDtypeStruct((R, R), jnp.float32),
        compiler_params=pltpu.CompilerParams(vmem_limit_bytes=4 * 1024 * 1024),
        cost_estimate=pl.CostEstimate(flops=10_000_000, bytes_accessed=32768, transcendentals=128),
    )(gram)


def apply_left(factor, m):
    return jnp.dot(factor, m, precision=HIGH, preferred_element_type=jnp.float32)


def partner(flip):
    return [(i, i ^ flip) for i in range(lax.axis_size("dp"))]


def feature_totals(part, first):
    n = part.shape[1]
    nz = lax.axis_size("dp") // 2
    small = n <= 512
    if small:
        blocks = part.reshape(2, R // 2, n)
    else:
        blocks = part.reshape(2, R // 16, 8, 2, n // 256, 128).transpose(0, 1, 3, 4, 2, 5)
        blocks = blocks.reshape(2, nz, n // 32, 128)
    first = first[: blocks.shape[-1]] == 1
    kept = jnp.where(first, blocks[0], blocks[1])
    sent = jnp.where(first, blocks[1], blocks[0])
    half = kept + lax.ppermute(sent, "dp", partner(1))
    if small:
        for flip in (2, 4, 14):
            half = half + lax.ppermute(half, "dp", partner(flip))
    else:
        groups = [[2 * z + c for z in range(nz)] for c in range(2)]
        own = added(lax.all_to_all(half, "dp", 0, 0, axis_index_groups=groups))
        own = jnp.broadcast_to(own[None], half.shape)
        half = lax.all_to_all(own, "dp", 0, 0, axis_index_groups=groups)
    other = lax.ppermute(half, "dp", partner(1))
    full = jnp.stack([jnp.where(first, half, other), jnp.where(first, other, half)])
    if small:
        return full.reshape(R, n)
    full = full.reshape(2, R // 16, 2, n // 256, 8, 128).transpose(0, 1, 4, 2, 3, 5)
    return full.reshape(R, n)


def per_device(acts, grads, sketch, picks):
    token_count_overall = picks.shape[0] * lax.axis_size("dp")
    core = lax.axis_index("dp") & 1
    first = jnp.full((512,), 1, jnp.int32) - core
    sketch, counts, first = lax.optimization_barrier((sketch, counts_of(picks), first))

    def to_features(proj, w):
        return feature_totals(times(proj * counts, w), first)

    proj, _ = token_totals(sketch, grads, False)
    range_t = to_features(proj, acts)
    for step in range(ITERS):
        proj, factor = token_totals(range_t, acts, True)
        co_range = to_features(apply_left(factor, proj), grads)
        proj, factor = token_totals(co_range, grads, True)
        range_t = to_features(apply_left(factor, proj), acts)
    proj, factor = token_totals(range_t, acts, True)
    proj, basis = lax.optimization_barrier((apply_left(factor, proj), apply_left(factor, range_t)))
    adapter_down_weight = to_features(proj, grads) / math.sqrt(token_count_overall)
    return (adapter_down_weight, basis * math.sqrt(MODEL_WIDTH))


def solution(mesh):
    return jax.shard_map(
        per_device,
        mesh=mesh,
        in_specs=(P("dp", "tensor"), P("dp", "tensor"), P(None, "tensor"), P("dp")),
        out_specs=(P(None, "tensor"), P(None, "tensor")),
        check_vma=False,
    )
```

```python
import math

import jax
import jax.numpy as jnp
from jax import lax
from jax.experimental import pallas as pl
from jax.experimental.pallas import tpu as pltpu
from jax.sharding import PartitionSpec as P

MODEL_WIDTH = 8192
ITERS = 2
R = 64
Z_ORDER = (0, 2, 4, 6, 7, 5, 3, 1)
HIGH = lax.Precision.HIGHEST


def pieces(m):
    hi = lax.reduce_precision(m, 8, 7)
    rest = m - hi
    mid = lax.reduce_precision(rest, 8, 7)
    low = rest - mid
    return jnp.concatenate([hi, mid, low], axis=0).astype(jnp.bfloat16)


def whole(out):
    return out[:R] + (out[R : 2 * R] + out[2 * R :])


def times_transposed(stack, w):
    return whole(
        lax.dot_general(stack, w, (((1,), (1,)), ((), ())), preferred_element_type=jnp.float32)
    )


def times(m, w):
    return whole(jnp.dot(pieces(m), w, preferred_element_type=jnp.float32))


def gram_of(stack):
    g = lax.dot_general(
        stack, stack, (((1,), (1,)), ((), ())), preferred_element_type=jnp.float32
    )
    part = [[g[R * i : R * i + R, R * j : R * j + R] for j in range(3)] for i in range(3)]
    small = (part[1][2] + part[2][1]) + part[2][2]
    middle = (part[0][2] + part[2][0]) + part[1][1]
    return part[0][0] + ((part[0][1] + part[1][0]) + (middle + small))


def added(blocks):
    terms = [blocks[i] for i in range(blocks.shape[0])]
    while len(terms) > 1:
        terms = [terms[i] + terms[i + 1] for i in range(0, len(terms), 2)]
    return terms[0]


def counts_of(picks):
    tok = picks.shape[0]
    high_at = (picks[None, :] // 128 == jnp.arange(tok // 128, dtype=jnp.int32)[:, None])
    low_at = (picks[:, None] % 128 == jnp.arange(128, dtype=jnp.int32)[None, :])
    found = jnp.dot(
        high_at.astype(jnp.bfloat16),
        low_at.astype(jnp.bfloat16),
        preferred_element_type=jnp.float32,
    )
    return found.reshape(1, tok)


def token_totals(m, w, with_gram):
    stack = pieces(m)
    prod = times_transposed(stack, w)
    n = prod.shape[1] // 128
    part = prod.reshape(R, n, 128).transpose(1, 0, 2)
    if with_gram:
        gram = gram_of(stack).reshape(n, R // n, R)
        gram = jnp.pad(gram, ((0, 0), (0, 8 - R // n), (0, 128 - R)))
        part = jnp.concatenate([part, gram], axis=1)
    mine = added(lax.all_to_all(part, "tensor", 0, 0))
    total = lax.all_to_all(jnp.broadcast_to(mine[None], part.shape), "tensor", 0, 0)
    prod = total[:, :R].transpose(1, 0, 2).reshape(R, n * 128)
    if not with_gram:
        return prod, None
    return prod, inverse_factor(total[:, R : R + R // n, :R].reshape(R, R))


def inverse_factor_kernel(gram_ref, out_ref):
    shape = (8, 2 * R)
    lanes = lax.broadcasted_iota(jnp.int32, shape, 1)
    sub = lax.broadcasted_iota(jnp.int32, shape, 0)
    n = R // 8
    tiles = []
    for i in range(n):
        tile = jnp.concatenate(
            [gram_ref[8 * i : 8 * i + 8, :], jnp.zeros((8, R), jnp.float32)], axis=1
        )
        tiles.append(jnp.where(lanes == sub + (R + 8 * i), 1.0, tile))

    def column(x, j):
        return jnp.broadcast_to(x[:, j : j + 1], shape)

    def row(x, j):
        return jnp.broadcast_to(x[j : j + 1, :], shape)

    for t in range(n):
        block = tiles[t]
        cols = [column(block, 8 * t + k) for k in range(8)]
        below = [[column(tiles[i], 8 * t + k) for k in range(8)] for i in range(t + 1, n)]
        out = block
        for s in range(8):
            here = sub == s
            pivot = row(cols[s], s)
            inv = 1.0 / pivot
            factor = cols[s] * inv
            for k in range(s + 1, 8):
                across = row(cols[k], s)
                cols[k] = jnp.where(here, across * inv, cols[k] - factor * across)
            across = row(block, s)
            out = jnp.where(here, across * lax.rsqrt(pivot), out)
            block = jnp.where(here, across * inv, block - factor * across)
        out_ref[8 * t : 8 * t + 8, :] = out[:, R:]
        rows = [row(block, k) for k in range(8)]
        for i in range(t + 1, n):
            terms = [c * r for c, r in zip(below[i - t - 1], rows)]
            while len(terms) > 1:
                terms = [terms[k] + terms[k + 1] for k in range(0, len(terms), 2)]
            tiles[i] = tiles[i] - terms[0]


def inverse_factor(gram):
    return pl.pallas_call(
        inverse_factor_kernel,
        out_shape=jax.ShapeDtypeStruct((R, R), jnp.float32),
        compiler_params=pltpu.CompilerParams(vmem_limit_bytes=4 * 1024 * 1024),
        cost_estimate=pl.CostEstimate(flops=10_000_000, bytes_accessed=32768, transcendentals=128),
    )(gram)


def apply_left(factor, m):
    return jnp.dot(factor, m, precision=HIGH, preferred_element_type=jnp.float32)


def partner(flip):
    return [(i, i ^ flip) for i in range(lax.axis_size("dp"))]


def feature_totals(part, firsts, factor, beside=None):
    n = part.shape[1]
    nz = len(Z_ORDER)
    small = n <= 512
    if small:
        blocks = part.reshape(2, R // 2, n)
    else:
        blocks = part.reshape(2, R // 16, 8, 2, n // 256, 128).transpose(0, 1, 3, 4, 2, 5)
        blocks = blocks.reshape(2, nz, n // 32, 128)
    first = firsts[blocks.shape[-1]]
    kept = jnp.where(first, blocks[0], blocks[1])
    sent = jnp.where(first, blocks[1], blocks[0])
    half = kept + lax.ppermute(sent, "dp", partner(1))
    if small:
        half = half + lax.ppermute(half, "dp", partner(2))
        near, across, far = [lax.ppermute(half, "dp", partner(2 * k)) for k in (2, 7, 5)]
        half = (half + near) + (far + across)
    else:
        if factor is not None:
            half, factor = lax.optimization_barrier((half, factor))
        groups = [[2 * z + c for z in Z_ORDER] for c in range(2)]
        own = added(lax.all_to_all(half, "dp", 0, 0, axis_index_groups=groups))
        own = jnp.broadcast_to(own[None], half.shape)
        half = lax.all_to_all(own, "dp", 0, 0, axis_index_groups=groups)
    if beside is not None:
        half, beside = lax.optimization_barrier((half, beside))
    other = lax.ppermute(half, "dp", partner(1))
    full = jnp.stack([jnp.where(first, half, other), jnp.where(first, other, half)])
    if small:
        full = full.reshape(R, n)
    else:
        full = full.reshape(2, R // 16, 2, n // 256, 8, 128).transpose(0, 1, 4, 2, 3, 5)
        full = full.reshape(R, n)
    return full if factor is None else apply_left(factor, full), beside


def per_device(acts, grads, sketch, picks):
    token_count_overall = picks.shape[0] * lax.axis_size("dp")
    first = jnp.full((512,), lax.axis_index("dp") & 1, jnp.int32) == 0
    sketch, counts, *first = lax.optimization_barrier(
        (sketch, counts_of(picks), first, first[:128])
    )
    firsts = {f.shape[0]: f for f in first}

    def to_features(proj, w, factor, beside=None):
        return feature_totals(times(proj * counts, w), firsts, factor, beside)

    proj, _ = token_totals(sketch, grads, False)
    range_t, _ = to_features(proj, acts, None)
    for step in range(ITERS):
        proj, factor = token_totals(range_t, acts, True)
        co_range, _ = to_features(proj, grads, factor)
        proj, factor = token_totals(co_range, grads, True)
        range_t, _ = to_features(proj, acts, factor)
    proj, factor = token_totals(range_t, acts, True)
    down, (factor, range_t) = to_features(proj, grads, factor, (factor, range_t))
    return (
        down / math.sqrt(token_count_overall),
        apply_left(factor, range_t) * math.sqrt(MODEL_WIDTH),
    )


def solution(mesh):
    return jax.shard_map(
        per_device,
        mesh=mesh,
        in_specs=(P("dp", "tensor"), P("dp", "tensor"), P(None, "tensor"), P("dp")),
        out_specs=(P(None, "tensor"), P(None, "tensor")),
        check_vma=False,
    )
```

```python
import math

import jax
import jax.numpy as jnp
from jax import lax
from jax.experimental import pallas as pl
from jax.experimental.pallas import tpu as pltpu
from jax.sharding import PartitionSpec as P

MODEL_WIDTH = 8192
ITERS = 2
R = 64
Z_ORDER = (0, 2, 4, 6, 7, 5, 3, 1)
HIGH = lax.Precision.HIGHEST


def pieces(m):
    hi = lax.reduce_precision(m, 8, 7)
    rest = m - hi
    mid = lax.reduce_precision(rest, 8, 7)
    low = rest - mid
    return jnp.concatenate([hi, mid, low], axis=0).astype(jnp.bfloat16)


def whole(out):
    return out[:R] + (out[R : 2 * R] + out[2 * R :])


def times_transposed(stack, w):
    return whole(
        lax.dot_general(stack, w, (((1,), (1,)), ((), ())), preferred_element_type=jnp.float32)
    )


def times(m, w):
    return whole(jnp.dot(pieces(m), w, preferred_element_type=jnp.float32))


def gram_of(stack):
    g = lax.dot_general(
        stack, stack, (((1,), (1,)), ((), ())), preferred_element_type=jnp.float32
    )
    part = [[g[R * i : R * i + R, R * j : R * j + R] for j in range(3)] for i in range(3)]
    small = (part[1][2] + part[2][1]) + part[2][2]
    middle = (part[0][2] + part[2][0]) + part[1][1]
    return part[0][0] + ((part[0][1] + part[1][0]) + (middle + small))


def added(blocks):
    terms = [blocks[i] for i in range(blocks.shape[0])]
    while len(terms) > 1:
        terms = [terms[i] + terms[i + 1] for i in range(0, len(terms), 2)]
    return terms[0]


def counts_of(picks):
    tok = picks.shape[0]
    high_at = (picks[None, :] >> 7 == jnp.arange(tok // 128, dtype=jnp.int32)[:, None])
    low_at = (picks[:, None] & 127 == jnp.arange(128, dtype=jnp.int32)[None, :])
    found = jnp.dot(
        high_at.astype(jnp.bfloat16),
        low_at.astype(jnp.bfloat16),
        preferred_element_type=jnp.float32,
    )
    return found.reshape(1, tok)


def core_kernel(out_ref):
    out_ref[...] = jnp.full(out_ref.shape, lax.axis_index("dp") & 1, jnp.int32)


def core_number():
    return pl.pallas_call(
        core_kernel,
        out_shape=jax.ShapeDtypeStruct((8, 512), jnp.int32),
        compiler_params=pltpu.CompilerParams(vmem_limit_bytes=4 * 1024 * 1024),
    )()


def token_totals(m, w, with_gram):
    stack = pieces(m)
    prod = times_transposed(stack, w)
    n = prod.shape[1] // 128
    part = prod.reshape(R, n, 128).transpose(1, 0, 2)
    if with_gram:
        gram = gram_of(stack).reshape(n, R // n, R)
        gram = jnp.pad(gram, ((0, 0), (0, 8 - R // n), (0, 128 - R)))
        part = jnp.concatenate([part, gram], axis=1)
    mine = added(lax.all_to_all(part, "tensor", 0, 0))
    total = lax.all_to_all(jnp.broadcast_to(mine[None], part.shape), "tensor", 0, 0)
    prod = total[:, :R].transpose(1, 0, 2).reshape(R, n * 128)
    if not with_gram:
        return prod, None
    return prod, inverse_factor(total[:, R : R + R // n, :R].reshape(R, R))


def inverse_factor_kernel(gram_ref, out_ref):
    shape = (8, 2 * R)
    lanes = lax.broadcasted_iota(jnp.int32, shape, 1)
    sub = lax.broadcasted_iota(jnp.int32, shape, 0)
    n = R // 8
    tiles = []
    for i in range(n):
        tile = jnp.concatenate(
            [gram_ref[8 * i : 8 * i + 8, :], jnp.zeros((8, R), jnp.float32)], axis=1
        )
        tiles.append(jnp.where(lanes == sub + (R + 8 * i), 1.0, tile))

    def column(x, j):
        return jnp.broadcast_to(x[:, j : j + 1], shape)

    def row(x, j):
        return jnp.broadcast_to(x[j : j + 1, :], shape)

    for t in range(n):
        block = tiles[t]
        cols = [column(block, 8 * t + k) for k in range(8)]
        below = [[column(tiles[i], 8 * t + k) for k in range(8)] for i in range(t + 1, n)]
        out = block
        for s in range(8):
            here = sub == s
            pivot = row(cols[s], s)
            inv = 1.0 / pivot
            factor = cols[s] * inv
            for k in range(s + 1, 8):
                across = row(cols[k], s)
                cols[k] = jnp.where(here, across * inv, cols[k] - factor * across)
            across = row(block, s)
            out = jnp.where(here, across * lax.rsqrt(pivot), out)
            block = jnp.where(here, across * inv, block - factor * across)
        out_ref[8 * t : 8 * t + 8, :] = out[:, R:]
        rows = [row(block, k) for k in range(8)]
        for i in range(t + 1, n):
            terms = [c * r for c, r in zip(below[i - t - 1], rows)]
            while len(terms) > 1:
                terms = [terms[k] + terms[k + 1] for k in range(0, len(terms), 2)]
            tiles[i] = tiles[i] - terms[0]


def inverse_factor(gram):
    return pl.pallas_call(
        inverse_factor_kernel,
        out_shape=jax.ShapeDtypeStruct((R, R), jnp.float32),
        compiler_params=pltpu.CompilerParams(vmem_limit_bytes=4 * 1024 * 1024),
        cost_estimate=pl.CostEstimate(flops=10_000_000, bytes_accessed=32768, transcendentals=128),
    )(gram)


def apply_left(factor, m):
    return jnp.dot(factor, m, precision=HIGH, preferred_element_type=jnp.float32)


def partner(flip):
    return [(i, i ^ flip) for i in range(lax.axis_size("dp"))]


def feature_totals(part, firsts, factor, beside=None):
    n = part.shape[1]
    nz = len(Z_ORDER)
    small = n <= 512
    if small:
        blocks = part.reshape(2, R // 2, n)
    else:
        blocks = part.reshape(2, R // 16, 8, 2, n // 256, 128).transpose(0, 1, 3, 4, 2, 5)
        blocks = blocks.reshape(2, nz, n // 32, 128)
    first = firsts[blocks.shape[-1]]
    kept = jnp.where(first, blocks[0], blocks[1])
    sent = jnp.where(first, blocks[1], blocks[0])
    half = kept + lax.ppermute(sent, "dp", partner(1))
    if small:
        half = half + lax.ppermute(half, "dp", partner(2))
        near, across, far = [lax.ppermute(half, "dp", partner(2 * k)) for k in (2, 7, 5)]
        half = (half + near) + (far + across)
    else:
        if factor is not None:
            half, factor = lax.optimization_barrier((half, factor))
        groups = [[2 * z + c for z in Z_ORDER] for c in range(2)]
        own = added(lax.all_to_all(half, "dp", 0, 0, axis_index_groups=groups))
        own = jnp.broadcast_to(own[None], half.shape)
        half = lax.all_to_all(own, "dp", 0, 0, axis_index_groups=groups)
    if small and factor is not None:
        half, factor = lax.optimization_barrier((half, factor))
    if beside is not None:
        half, beside = lax.optimization_barrier((half, beside))
    other = lax.ppermute(half, "dp", partner(1))
    full = jnp.stack([jnp.where(first, half, other), jnp.where(first, other, half)])
    if small:
        full = full.reshape(R, n)
    else:
        full = full.reshape(2, R // 16, 2, n // 256, 8, 128).transpose(0, 1, 4, 2, 3, 5)
        full = full.reshape(R, n)
    return full if factor is None else apply_left(factor, full), beside


def per_device(acts, grads, sketch, picks):
    token_count_overall = picks.shape[0] * lax.axis_size("dp")
    first = core_number()[0] == 0
    sketch, counts, *first = lax.optimization_barrier(
        (sketch, counts_of(picks), first, first[:128])
    )
    firsts = {f.shape[0]: f for f in first}

    def to_features(proj, w, factor, beside=None):
        return feature_totals(times(proj * counts, w), firsts, factor, beside)

    proj, _ = token_totals(sketch, grads, False)
    range_t, _ = to_features(proj, acts, None)
    for step in range(ITERS):
        proj, factor = token_totals(range_t, acts, True)
        co_range, _ = to_features(proj, grads, factor)
        proj, factor = token_totals(co_range, grads, True)
        range_t, _ = to_features(proj, acts, factor)
    proj, factor = token_totals(range_t, acts, True)
    down, (factor, range_t) = to_features(proj, grads, factor, (factor, range_t))
    return (
        down / math.sqrt(token_count_overall),
        apply_left(factor, range_t) * math.sqrt(MODEL_WIDTH),
    )


def solution(mesh):
    return jax.shard_map(
        per_device,
        mesh=mesh,
        in_specs=(P("dp", "tensor"), P("dp", "tensor"), P(None, "tensor"), P("dp")),
        out_specs=(P(None, "tensor"), P(None, "tensor")),
        check_vma=False,
    )
```

```python
import math

import jax
import jax.numpy as jnp
from jax import lax
from jax.experimental import pallas as pl
from jax.experimental.pallas import tpu as pltpu
from jax.sharding import PartitionSpec as P

MODEL_WIDTH = 8192
ITERS = 2
R = 64
FIRST_ROWS = 768
UPPER = 32
Z_ORDER = (0, 2, 4, 6, 7, 5, 3, 1)
HIGH = lax.Precision.HIGHEST


def pieces(m):
    hi = lax.reduce_precision(m, 8, 7)
    rest = m - hi
    mid = lax.reduce_precision(rest, 8, 7)
    low = rest - mid
    return jnp.concatenate([hi, mid, low], axis=0).astype(jnp.bfloat16)


def whole(out):
    return out[:R] + (out[R : 2 * R] + out[2 * R :])


def times_transposed(stack, w):
    return whole(
        lax.dot_general(stack, w, (((1,), (1,)), ((), ())), preferred_element_type=jnp.float32)
    )


def times(m, w):
    return whole(jnp.dot(pieces(m), w, preferred_element_type=jnp.float32))


def gram_of(stack):
    g = lax.dot_general(
        stack, stack, (((1,), (1,)), ((), ())), preferred_element_type=jnp.float32
    )
    part = [[g[R * i : R * i + R, R * j : R * j + R] for j in range(3)] for i in range(3)]
    small = (part[1][2] + part[2][1]) + part[2][2]
    middle = (part[0][2] + part[2][0]) + part[1][1]
    return part[0][0] + ((part[0][1] + part[1][0]) + (middle + small))


def added(blocks):
    terms = [blocks[i] for i in range(blocks.shape[0])]
    while len(terms) > 1:
        terms = [terms[i] + terms[i + 1] for i in range(0, len(terms), 2)]
    return terms[0]


def counts_of(picks):
    tok = picks.shape[0]
    high_at = (picks[None, :] >> 7 == jnp.arange(tok // 128, dtype=jnp.int32)[:, None])
    low_at = (picks[:, None] & 127 == jnp.arange(128, dtype=jnp.int32)[None, :])
    found = jnp.dot(
        high_at.astype(jnp.bfloat16),
        low_at.astype(jnp.bfloat16),
        preferred_element_type=jnp.float32,
    )
    return found.reshape(1, tok)


def core_kernel(out_ref):
    out_ref[...] = jnp.full(out_ref.shape, lax.axis_index("dp") & 1, jnp.int32)


def core_number():
    return pl.pallas_call(
        core_kernel,
        out_shape=jax.ShapeDtypeStruct((8, 512), jnp.int32),
        compiler_params=pltpu.CompilerParams(vmem_limit_bytes=4 * 1024 * 1024),
    )()


def token_totals(m, w, with_gram):
    stack = pieces(m)
    if with_gram:
        prod = times_transposed(stack, w)
    else:
        prod = jnp.concatenate(
            [times_transposed(stack, w[:FIRST_ROWS]), times_transposed(stack, w[FIRST_ROWS:])],
            axis=1,
        )
    n = prod.shape[1] // 128
    part = prod.reshape(R, n, 128).transpose(1, 0, 2)
    if with_gram:
        gram = gram_of(stack).reshape(n, R // n, R)
        gram = jnp.pad(gram, ((0, 0), (0, 8 - R // n), (0, 128 - R)))
        part = jnp.concatenate([part, gram], axis=1)
    mine = added(lax.all_to_all(part, "tensor", 0, 0))
    total = lax.all_to_all(jnp.broadcast_to(mine[None], part.shape), "tensor", 0, 0)
    prod = total[:, :R].transpose(1, 0, 2).reshape(R, n * 128)
    if not with_gram:
        return prod, None
    return prod, total[:, R : R + R // n, :R].reshape(R, R)


def eliminate(tiles, first, last, out_ref):
    shape = (8, 2 * R)
    sub = lax.broadcasted_iota(jnp.int32, shape, 0)
    n = R // 8

    def column(x, j):
        return jnp.broadcast_to(x[:, j : j + 1], shape)

    def row(x, j):
        return jnp.broadcast_to(x[j : j + 1, :], shape)

    for t in range(first, last):
        block = tiles[t]
        cols = [column(block, 8 * t + k) for k in range(8)]
        below = [[column(tiles[i], 8 * t + k) for k in range(8)] for i in range(t + 1, n)]
        out = block
        for s in range(8):
            here = sub == s
            pivot = row(cols[s], s)
            inv = 1.0 / pivot
            factor = cols[s] * inv
            for k in range(s + 1, 8):
                across = row(cols[k], s)
                cols[k] = jnp.where(here, across * inv, cols[k] - factor * across)
            across = row(block, s)
            out = jnp.where(here, across * lax.rsqrt(pivot), out)
            block = jnp.where(here, across * inv, block - factor * across)
        out_ref[8 * t : 8 * t + 8, :] = out[:, R:]
        rows = [row(block, k) for k in range(8)]
        for i in range(t + 1, n):
            terms = [c * r for c, r in zip(below[i - t - 1], rows)]
            while len(terms) > 1:
                terms = [terms[k] + terms[k + 1] for k in range(0, len(terms), 2)]
            tiles[i] = tiles[i] - terms[0]


def upper_rows_kernel(gram_ref, out_ref, rest_ref):
    lanes = lax.broadcasted_iota(jnp.int32, (8, 2 * R), 1)
    sub = lax.broadcasted_iota(jnp.int32, (8, 2 * R), 0)
    tiles = []
    for i in range(R // 8):
        tile = jnp.concatenate(
            [gram_ref[8 * i : 8 * i + 8, :], jnp.zeros((8, R), jnp.float32)], axis=1
        )
        tiles.append(jnp.where(lanes == sub + (R + 8 * i), 1.0, tile))
    eliminate(tiles, 0, UPPER // 8, out_ref)
    for i in range(UPPER // 8, R // 8):
        rest_ref[8 * i - UPPER : 8 * i - UPPER + 8, :] = tiles[i]


def lower_rows_kernel(upper_ref, rest_ref, out_ref):
    out_ref[:UPPER, :] = upper_ref[...]
    tiles = [None] * (UPPER // 8)
    tiles += [rest_ref[8 * i : 8 * i + 8, :] for i in range((R - UPPER) // 8)]
    eliminate(tiles, UPPER // 8, R // 8, out_ref)


FACTOR_PARAMS = {
    "compiler_params": pltpu.CompilerParams(vmem_limit_bytes=4 * 1024 * 1024),
    "cost_estimate": pl.CostEstimate(flops=5_000_000, bytes_accessed=32768, transcendentals=64),
}


def upper_rows(gram):
    return pl.pallas_call(
        upper_rows_kernel,
        out_shape=[
            jax.ShapeDtypeStruct((UPPER, R), jnp.float32),
            jax.ShapeDtypeStruct((R - UPPER, 2 * R), jnp.float32),
        ],
        **FACTOR_PARAMS,
    )(gram)


def lower_rows(begun):
    return pl.pallas_call(
        lower_rows_kernel,
        out_shape=jax.ShapeDtypeStruct((R, R), jnp.float32),
        **FACTOR_PARAMS,
    )(*begun)


def apply_left(factor, m):
    return jnp.dot(factor, m, precision=HIGH, preferred_element_type=jnp.float32)


def partner(flip):
    return [(i, i ^ flip) for i in range(lax.axis_size("dp"))]


def along_ring(step):
    nz = len(Z_ORDER)
    sources = [(z + step if z % 2 == 0 else z - step) % nz for z in range(nz)]
    return [(2 * sources[z] + c, 2 * z + c) for z in range(nz) for c in range(2)]


def feature_totals(part, firsts, gram, range_t=None):
    n = part.shape[1]
    nz = len(Z_ORDER)
    small = n <= 512
    if small:
        blocks = part.reshape(2, R // 2, n)
    else:
        blocks = part.reshape(2, R // 16, 8, 2, n // 256, 128).transpose(0, 1, 3, 4, 2, 5)
        blocks = blocks.reshape(2, nz, n // 32, 128)
    first = firsts[blocks.shape[-1]]
    kept = jnp.where(first, blocks[0], blocks[1])
    sent = jnp.where(first, blocks[1], blocks[0])
    half = kept + lax.ppermute(sent, "dp", partner(1))
    begun = factor = None
    if gram is not None:
        begun = upper_rows(gram)
        if small or range_t is not None:
            factor = lower_rows(begun)
    if small:
        half = half + lax.ppermute(half, "dp", partner(2))
        near, next_near, far = [lax.ppermute(half, "dp", along_ring(k)) for k in (-1, 2, -3)]
        half = (half + far) + (near + next_near)
    else:
        half, begun, factor = lax.optimization_barrier((half, begun, factor))
        groups = [[2 * z + c for z in Z_ORDER] for c in range(2)]
        own = added(lax.all_to_all(half, "dp", 0, 0, axis_index_groups=groups))
        own = jnp.broadcast_to(own[None], half.shape)
        half = lax.all_to_all(own, "dp", 0, 0, axis_index_groups=groups)
    half, begun, factor, range_t = lax.optimization_barrier((half, begun, factor, range_t))
    if gram is not None and factor is None:
        factor = lower_rows(begun)
    other = lax.ppermute(half, "dp", partner(1))
    full = jnp.stack([jnp.where(first, half, other), jnp.where(first, other, half)])
    if small:
        full = full.reshape(R, n)
    else:
        full = full.reshape(2, R // 16, 2, n // 256, 8, 128).transpose(0, 1, 4, 2, 3, 5)
        full = full.reshape(R, n)
    if gram is None:
        return full
    full = apply_left(factor, full)
    return full if range_t is None else (full, apply_left(factor, range_t))


def per_device(acts, grads, sketch, picks):
    token_count_overall = picks.shape[0] * lax.axis_size("dp")
    first = core_number()[0] == 0
    sketch, counts, *first = lax.optimization_barrier(
        (sketch, counts_of(picks), first, first[:128])
    )
    firsts = {f.shape[0]: f for f in first}

    def to_features(proj, w, gram, range_t=None):
        return feature_totals(times(proj * counts, w), firsts, gram, range_t)

    proj, _ = token_totals(sketch, grads, False)
    range_t = to_features(proj, acts, None)
    for step in range(ITERS):
        proj, gram = token_totals(range_t, acts, True)
        co_range = to_features(proj, grads, gram)
        proj, gram = token_totals(co_range, grads, True)
        range_t = to_features(proj, acts, gram)
    proj, gram = token_totals(range_t, acts, True)
    down, basis = to_features(proj, grads, gram, range_t)
    return (down / math.sqrt(token_count_overall), basis * math.sqrt(MODEL_WIDTH))


def solution(mesh):
    return jax.shard_map(
        per_device,
        mesh=mesh,
        in_specs=(P("dp", "tensor"), P("dp", "tensor"), P(None, "tensor"), P("dp")),
        out_specs=(P(None, "tensor"), P(None, "tensor")),
        check_vma=False,
    )
```

```python
import math

import jax
import jax.numpy as jnp
from jax import lax
from jax.experimental import pallas as pl
from jax.experimental.pallas import tpu as pltpu
from jax.sharding import PartitionSpec as P

MODEL_WIDTH = 8192
ITERS = 2
R = 64
FIRST_ROWS = 768
NZ = 8
HIGH = lax.Precision.HIGHEST


def pieces(m):
    hi = lax.reduce_precision(m, 8, 7)
    rest = m - hi
    mid = lax.reduce_precision(rest, 8, 7)
    low = rest - mid
    return jnp.concatenate([hi, mid, low], axis=0).astype(jnp.bfloat16)


def whole(out):
    return out[:R] + (out[R : 2 * R] + out[2 * R :])


def times_transposed(stack, w):
    return whole(
        lax.dot_general(stack, w, (((1,), (1,)), ((), ())), preferred_element_type=jnp.float32)
    )


def times(m, w):
    return whole(jnp.dot(pieces(m), w, preferred_element_type=jnp.float32))


def gram_of(stack):
    g = lax.dot_general(
        stack, stack, (((1,), (1,)), ((), ())), preferred_element_type=jnp.float32
    )
    part = [[g[R * i : R * i + R, R * j : R * j + R] for j in range(3)] for i in range(3)]
    small = (part[1][2] + part[2][1]) + part[2][2]
    middle = (part[0][2] + part[2][0]) + part[1][1]
    return part[0][0] + ((part[0][1] + part[1][0]) + (middle + small))


def added(blocks):
    terms = [blocks[i] for i in range(blocks.shape[0])]
    while len(terms) > 1:
        terms = [terms[i] + terms[i + 1] for i in range(0, len(terms), 2)]
    return terms[0]


def counts_of(picks):
    tok = picks.shape[0]
    high_at = (picks[None, :] >> 7 == jnp.arange(tok // 128, dtype=jnp.int32)[:, None])
    low_at = (picks[:, None] & 127 == jnp.arange(128, dtype=jnp.int32)[None, :])
    found = jnp.dot(
        high_at.astype(jnp.bfloat16),
        low_at.astype(jnp.bfloat16),
        preferred_element_type=jnp.float32,
    )
    return found.reshape(1, tok)


def place_kernel(out_ref):
    place = lax.axis_index("dp")
    z = place >> 1
    which = lax.broadcasted_iota(jnp.int32, out_ref.shape, 0)
    out_ref[...] = jnp.where(which == 0, place & 1, (z ^ (z >> 2)) & 1)


def place_numbers(n):
    return pl.pallas_call(
        place_kernel,
        out_shape=jax.ShapeDtypeStruct((8, n), jnp.int32),
        compiler_params=pltpu.CompilerParams(vmem_limit_bytes=4 * 1024 * 1024),
    )()


def token_totals(m, w, with_gram):
    stack = pieces(m)
    if with_gram:
        prod = times_transposed(stack, w)
    else:
        prod = jnp.concatenate(
            [times_transposed(stack, w[:FIRST_ROWS]), times_transposed(stack, w[FIRST_ROWS:])],
            axis=1,
        )
    n = prod.shape[1] // 128
    part = prod.reshape(R, n, 128).transpose(1, 0, 2)
    if with_gram:
        gram = gram_of(stack).reshape(n, R // n, R)
        gram = jnp.pad(gram, ((0, 0), (0, 8 - R // n), (0, 128 - R)))
        part = jnp.concatenate([part, gram], axis=1)
    mine = added(lax.all_to_all(part, "tensor", 0, 0))
    total = lax.all_to_all(jnp.broadcast_to(mine[None], part.shape), "tensor", 0, 0)
    prod = total[:, :R].transpose(1, 0, 2).reshape(R, n * 128)
    if not with_gram:
        return prod, None
    return prod, total[:, R : R + R // n, :R].reshape(R, R)


def inverse_factor_kernel(gram_ref, out_ref):
    shape = (8, 2 * R)
    lanes = lax.broadcasted_iota(jnp.int32, shape, 1)
    sub = lax.broadcasted_iota(jnp.int32, shape, 0)
    n = R // 8
    tiles = []
    for i in range(n):
        tile = jnp.concatenate(
            [gram_ref[8 * i : 8 * i + 8, :], jnp.zeros((8, R), jnp.float32)], axis=1
        )
        tiles.append(jnp.where(lanes == sub + (R + 8 * i), 1.0, tile))

    def column(x, j):
        return jnp.broadcast_to(x[:, j : j + 1], shape)

    def row(x, j):
        return jnp.broadcast_to(x[j : j + 1, :], shape)

    for t in range(n):
        block = tiles[t]
        cols = [column(block, 8 * t + k) for k in range(8)]
        below = [[column(tiles[i], 8 * t + k) for k in range(8)] for i in range(t + 1, n)]
        out = block
        for s in range(8):
            here = sub == s
            pivot = row(cols[s], s)
            inv = 1.0 / pivot
            factor = cols[s] * inv
            for k in range(s + 1, 8):
                across = row(cols[k], s)
                cols[k] = jnp.where(here, across * inv, cols[k] - factor * across)
            across = row(block, s)
            out = jnp.where(here, across * lax.rsqrt(pivot), out)
            block = jnp.where(here, across * inv, block - factor * across)
        out_ref[8 * t : 8 * t + 8, :] = out[:, R:]
        rows = [row(block, k) for k in range(8)]
        for i in range(t + 1, n):
            terms = [c * r for c, r in zip(below[i - t - 1], rows)]
            while len(terms) > 1:
                terms = [terms[k] + terms[k + 1] for k in range(0, len(terms), 2)]
            tiles[i] = tiles[i] - terms[0]


def inverse_factor(gram):
    return pl.pallas_call(
        inverse_factor_kernel,
        out_shape=jax.ShapeDtypeStruct((R, R), jnp.float32),
        compiler_params=pltpu.CompilerParams(vmem_limit_bytes=4 * 1024 * 1024),
        cost_estimate=pl.CostEstimate(flops=10_000_000, bytes_accessed=32768, transcendentals=128),
    )(gram)


def apply_left(factor, m):
    return jnp.dot(factor, m, precision=HIGH, preferred_element_type=jnp.float32)


def partner(flip):
    return [(i, i ^ flip) for i in range(lax.axis_size("dp"))]


def along_ring(step):
    sources = [(z + step if z % 2 == 0 else z - step) % NZ for z in range(NZ)]
    return [(2 * sources[z] + c, 2 * z + c) for z in range(NZ) for c in range(2)]


def feature_totals(part, firsts, gram, range_t=None):
    n = part.shape[1]
    first_core, first_part = (f[:n] for f in firsts)
    half = part.reshape(2, R // 2, n)
    kept = jnp.where(first_core, half[0], half[1])
    sent = jnp.where(first_core, half[1], half[0])
    half = kept + lax.ppermute(sent, "dp", partner(1))
    factor = None if gram is None else inverse_factor(gram)
    if n <= 512:
        half = half + lax.ppermute(half, "dp", partner(2))
        near, next_near, far = [lax.ppermute(half, "dp", along_ring(k)) for k in (-1, 2, -3)]
        half = (half + far) + (near + next_near)
    else:
        quarter = half.reshape(2, R // 4, n)
        kept = jnp.where(first_part, quarter[0], quarter[1])
        sent = jnp.where(first_part, quarter[1], quarter[0])
        mine = kept + lax.ppermute(sent, "dp", partner(2))
        near, across, far = [lax.ppermute(mine, "dp", partner(2 * k)) for k in (2, 7, 5)]
        mine = (mine + near) + (far + across)
        if factor is not None:
            mine, factor = lax.optimization_barrier((mine, factor))
        other = lax.ppermute(mine, "dp", partner(2))
        half = jnp.concatenate(
            [jnp.where(first_part, mine, other), jnp.where(first_part, other, mine)], axis=0
        )
    if factor is not None:
        half, factor = lax.optimization_barrier((half, factor))
    other = lax.ppermute(half, "dp", partner(1))
    full = jnp.concatenate(
        [jnp.where(first_core, half, other), jnp.where(first_core, other, half)], axis=0
    )
    if factor is None:
        return full
    full = apply_left(factor, full)
    return full if range_t is None else (full, apply_left(factor, range_t))


def per_device(acts, grads, sketch, picks):
    token_count_overall = picks.shape[0] * lax.axis_size("dp")
    place = place_numbers(sketch.shape[1])
    sketch, counts, *firsts = lax.optimization_barrier(
        (sketch, counts_of(picks), place[0] == 0, place[1] == 0)
    )

    def to_features(proj, w, gram, range_t=None):
        return feature_totals(times(proj * counts, w), firsts, gram, range_t)

    proj, _ = token_totals(sketch, grads, False)
    range_t = to_features(proj, acts, None)
    for step in range(ITERS):
        proj, gram = token_totals(range_t, acts, True)
        co_range = to_features(proj, grads, gram)
        proj, gram = token_totals(co_range, grads, True)
        range_t = to_features(proj, acts, gram)
    proj, gram = token_totals(range_t, acts, True)
    down, basis = to_features(proj, grads, gram, range_t)
    return (down / math.sqrt(token_count_overall), basis * math.sqrt(MODEL_WIDTH))


def solution(mesh):
    return jax.shard_map(
        per_device,
        mesh=mesh,
        in_specs=(P("dp", "tensor"), P("dp", "tensor"), P(None, "tensor"), P("dp")),
        out_specs=(P(None, "tensor"), P(None, "tensor")),
        check_vma=False,
    )
```

```python
import math

import jax
import jax.numpy as jnp
from jax import lax
from jax.experimental import pallas as pl
from jax.experimental.pallas import tpu as pltpu
from jax.sharding import PartitionSpec as P

MODEL_WIDTH = 8192
ITERS = 2
R = 64
FIRST_ROWS = 768
NZ = 8
HIGH = lax.Precision.HIGHEST


def pieces(m):
    hi = lax.reduce_precision(m, 8, 7)
    rest = m - hi
    mid = lax.reduce_precision(rest, 8, 7)
    low = rest - mid
    return jnp.concatenate([hi, mid, low], axis=0).astype(jnp.bfloat16)


def whole(out):
    return out[:R] + (out[R : 2 * R] + out[2 * R :])


def times_transposed(stack, w):
    return whole(
        lax.dot_general(stack, w, (((1,), (1,)), ((), ())), preferred_element_type=jnp.float32)
    )


def times(m, w):
    return whole(jnp.dot(pieces(m), w, preferred_element_type=jnp.float32))


def gram_of(stack):
    g = lax.dot_general(
        stack, stack, (((1,), (1,)), ((), ())), preferred_element_type=jnp.float32
    )
    part = [[g[R * i : R * i + R, R * j : R * j + R] for j in range(3)] for i in range(3)]
    small = (part[1][2] + part[2][1]) + part[2][2]
    middle = (part[0][2] + part[2][0]) + part[1][1]
    return part[0][0] + ((part[0][1] + part[1][0]) + (middle + small))


def added(blocks):
    terms = [blocks[i] for i in range(blocks.shape[0])]
    while len(terms) > 1:
        terms = [terms[i] + terms[i + 1] for i in range(0, len(terms), 2)]
    return terms[0]


def counts_of(picks):
    tok = picks.shape[0]
    high_at = (picks[None, :] >> 7 == jnp.arange(tok // 128, dtype=jnp.int32)[:, None])
    low_at = (picks[:, None] & 127 == jnp.arange(128, dtype=jnp.int32)[None, :])
    found = jnp.dot(
        high_at.astype(jnp.bfloat16),
        low_at.astype(jnp.bfloat16),
        preferred_element_type=jnp.float32,
    )
    return found.reshape(1, tok)


def place_kernel(out_ref):
    place = lax.axis_index("dp")
    z = place >> 1
    which = lax.broadcasted_iota(jnp.int32, out_ref.shape, 0)
    out_ref[...] = jnp.where(which == 0, place & 1, (z ^ (z >> 2)) & 1)


def place_numbers(n):
    return pl.pallas_call(
        place_kernel,
        out_shape=jax.ShapeDtypeStruct((8, n), jnp.int32),
        compiler_params=pltpu.CompilerParams(vmem_limit_bytes=4 * 1024 * 1024),
    )()


def token_totals(m, w, with_gram):
    stack = pieces(m)
    if with_gram:
        prod = times_transposed(stack, w)
    else:
        prod = jnp.concatenate(
            [times_transposed(stack, w[:FIRST_ROWS]), times_transposed(stack, w[FIRST_ROWS:])],
            axis=1,
        )
    n = prod.shape[1] // 128
    part = prod.reshape(R, n, 128).transpose(1, 0, 2)
    if with_gram:
        gram = gram_of(stack).reshape(n, R // n, R)
        gram = jnp.pad(gram, ((0, 0), (0, 8 - R // n), (0, 128 - R)))
        part = jnp.concatenate([part, gram], axis=1)
    mine = added(lax.all_to_all(part, "tensor", 0, 0))
    total = lax.all_to_all(jnp.broadcast_to(mine[None], part.shape), "tensor", 0, 0)
    prod = total[:, :R].transpose(1, 0, 2).reshape(R, n * 128)
    if not with_gram:
        return prod, None
    return prod, total[:, R : R + R // n, :R].reshape(R, R)


def inverse_factor_kernel(gram_ref, out_ref):
    shape = (8, 2 * R)
    lanes = lax.broadcasted_iota(jnp.int32, shape, 1)
    sub = lax.broadcasted_iota(jnp.int32, shape, 0)
    n = R // 8
    tiles = []
    for i in range(n):
        tile = jnp.concatenate(
            [gram_ref[8 * i : 8 * i + 8, :], jnp.zeros((8, R), jnp.float32)], axis=1
        )
        tiles.append(jnp.where(lanes == sub + (R + 8 * i), 1.0, tile))

    def column(x, j):
        return jnp.broadcast_to(x[:, j : j + 1], shape)

    def row(x, j):
        return jnp.broadcast_to(x[j : j + 1, :], shape)

    for t in range(n):
        block = tiles[t]
        cols = [column(block, 8 * t + k) for k in range(8)]
        below = [[column(tiles[i], 8 * t + k) for k in range(8)] for i in range(t + 1, n)]
        out = block
        for s in range(8):
            here = sub == s
            pivot = row(cols[s], s)
            inv = 1.0 / pivot
            factor = cols[s] * inv
            for k in range(s + 1, 8):
                across = row(cols[k], s)
                cols[k] = jnp.where(here, across * inv, cols[k] - factor * across)
            across = row(block, s)
            out = jnp.where(here, across * lax.rsqrt(pivot), out)
            block = jnp.where(here, across * inv, block - factor * across)
        out_ref[8 * t : 8 * t + 8, :] = out[:, R:]
        rows = [row(block, k) for k in range(8)]
        for i in range(t + 1, n):
            terms = [c * r for c, r in zip(below[i - t - 1], rows)]
            while len(terms) > 1:
                terms = [terms[k] + terms[k + 1] for k in range(0, len(terms), 2)]
            tiles[i] = tiles[i] - terms[0]


def inverse_factor(gram):
    return pl.pallas_call(
        inverse_factor_kernel,
        out_shape=jax.ShapeDtypeStruct((R, R), jnp.float32),
        compiler_params=pltpu.CompilerParams(vmem_limit_bytes=4 * 1024 * 1024),
        cost_estimate=pl.CostEstimate(flops=10_000_000, bytes_accessed=32768, transcendentals=128),
    )(gram)


def apply_left(factor, m):
    return jnp.dot(factor, m, precision=HIGH, preferred_element_type=jnp.float32)


def partner(flip):
    return [(i, i ^ flip) for i in range(lax.axis_size("dp"))]


def along_ring(step):
    sources = [(z + step if z % 2 == 0 else z - step) % NZ for z in range(NZ)]
    return [(2 * sources[z] + c, 2 * z + c) for z in range(NZ) for c in range(2)]


def feature_totals(part, firsts, gram, range_t=None):
    n = part.shape[1]
    first_core, first_part = (f[:n] for f in firsts)
    half = part.reshape(2, R // 2, n)
    kept = jnp.where(first_core, half[0], half[1])
    sent = jnp.where(first_core, half[1], half[0])
    half = kept + lax.ppermute(sent, "dp", partner(1))
    factor = None if gram is None else inverse_factor(gram)
    if n <= 512:
        half = half + lax.ppermute(half, "dp", partner(2))
        near, next_near, far = [lax.ppermute(half, "dp", along_ring(k)) for k in (-1, 2, -3)]
        half = (half + far) + (near + next_near)
    else:
        quarter = half.reshape(2, R // 4, n)
        kept = jnp.where(first_part, quarter[0], quarter[1])
        sent = jnp.where(first_part, quarter[1], quarter[0])
        mine = kept + lax.ppermute(sent, "dp", partner(2))
        near, across, far = [lax.ppermute(mine, "dp", partner(2 * k)) for k in (2, 7, 5)]
        mine = (mine + near) + (far + across)
        if factor is not None:
            mine, factor = lax.optimization_barrier((mine, factor))
        other = lax.ppermute(mine, "dp", partner(2))
        half = jnp.concatenate(
            [jnp.where(first_part, mine, other), jnp.where(first_part, other, mine)], axis=0
        )
    if factor is not None:
        half, factor = lax.optimization_barrier((half, factor))
    other = lax.ppermute(half, "dp", partner(1))
    full = jnp.concatenate(
        [jnp.where(first_core, half, other), jnp.where(first_core, other, half)], axis=0
    )
    if factor is None:
        return full
    full = apply_left(factor, full)
    return full if range_t is None else (full, apply_left(factor, range_t))


def per_device(acts, grads, sketch, picks):
    token_count_overall = picks.shape[0] * lax.axis_size("dp")
    place = place_numbers(sketch.shape[1])
    sketch, counts, *firsts = lax.optimization_barrier(
        (sketch, counts_of(picks), place[0] == 0, place[1] == 0)
    )

    def to_features(proj, w, gram, range_t=None):
        return feature_totals(times(proj * counts, w), firsts, gram, range_t)

    proj, _ = token_totals(sketch, grads, False)
    range_t = to_features(proj, acts, None)
    for step in range(ITERS):
        proj, gram = token_totals(range_t, acts, True)
        if step == 0:
            proj, gram = apply_left(inverse_factor(gram), proj), None
        co_range = to_features(proj, grads, gram)
        proj, gram = token_totals(co_range, grads, True)
        range_t = to_features(proj, acts, gram)
    proj, gram = token_totals(range_t, acts, True)
    down, basis = to_features(proj, grads, gram, range_t)
    return (down / math.sqrt(token_count_overall), basis * math.sqrt(MODEL_WIDTH))


def solution(mesh):
    return jax.shard_map(
        per_device,
        mesh=mesh,
        in_specs=(P("dp", "tensor"), P("dp", "tensor"), P(None, "tensor"), P("dp")),
        out_specs=(P(None, "tensor"), P(None, "tensor")),
        check_vma=False,
    )
```

```python
import math

import jax
import jax.numpy as jnp
from jax import lax
from jax.experimental import pallas as pl
from jax.experimental.pallas import tpu as pltpu
from jax.sharding import PartitionSpec as P

MODEL_WIDTH = 8192
ITERS = 2
R = 64
FIRST_ROWS = 768
NZ = 8
HIGH = lax.Precision.HIGHEST


def pieces(m):
    hi = lax.reduce_precision(m, 8, 7)
    rest = m - hi
    mid = lax.reduce_precision(rest, 8, 7)
    low = rest - mid
    return jnp.concatenate([hi, mid, low], axis=0).astype(jnp.bfloat16)


def whole(out):
    return out[:R] + (out[R : 2 * R] + out[2 * R :])


def times_transposed(stack, w):
    return whole(
        lax.dot_general(stack, w, (((1,), (1,)), ((), ())), preferred_element_type=jnp.float32)
    )


def times(m, w):
    return whole(jnp.dot(pieces(m), w, preferred_element_type=jnp.float32))


def gram_of(stack):
    g = lax.dot_general(
        stack, stack, (((1,), (1,)), ((), ())), preferred_element_type=jnp.float32
    )
    part = [[g[R * i : R * i + R, R * j : R * j + R] for j in range(3)] for i in range(3)]
    small = (part[1][2] + part[2][1]) + part[2][2]
    middle = (part[0][2] + part[2][0]) + part[1][1]
    return part[0][0] + ((part[0][1] + part[1][0]) + (middle + small))


def added(blocks):
    terms = [blocks[i] for i in range(blocks.shape[0])]
    while len(terms) > 1:
        terms = [terms[i] + terms[i + 1] for i in range(0, len(terms), 2)]
    return terms[0]


def counts_of(picks):
    tok = picks.shape[0]
    high_at = (picks[None, :] >> 7 == jnp.arange(tok // 128, dtype=jnp.int32)[:, None])
    low_at = (picks[:, None] & 127 == jnp.arange(128, dtype=jnp.int32)[None, :])
    found = jnp.dot(
        high_at.astype(jnp.bfloat16),
        low_at.astype(jnp.bfloat16),
        preferred_element_type=jnp.float32,
    )
    return found.reshape(1, tok)


def place_kernel(out_ref):
    place = lax.axis_index("dp")
    z = place >> 1
    which = lax.broadcasted_iota(jnp.int32, out_ref.shape, 0)
    out_ref[...] = jnp.where(which == 0, place & 1, (z ^ (z >> 2)) & 1)


def place_numbers(n):
    return pl.pallas_call(
        place_kernel,
        out_shape=jax.ShapeDtypeStruct((8, n), jnp.int32),
        compiler_params=pltpu.CompilerParams(vmem_limit_bytes=4 * 1024 * 1024),
    )()


def token_totals(m, w, with_gram):
    stack = pieces(m) if with_gram else m
    if with_gram:
        prod = times_transposed(stack, w)
    else:
        prod = jnp.concatenate(
            [times_transposed(stack, w[:FIRST_ROWS]), times_transposed(stack, w[FIRST_ROWS:])],
            axis=1,
        )
    n = prod.shape[1] // 128
    part = prod.reshape(R, n, 128).transpose(1, 0, 2)
    if with_gram:
        gram = gram_of(stack).reshape(n, R // n, R)
        gram = jnp.pad(gram, ((0, 0), (0, 8 - R // n), (0, 128 - R)))
        part = jnp.concatenate([part, gram], axis=1)
    mine = added(lax.all_to_all(part, "tensor", 0, 0))
    total = lax.all_to_all(jnp.broadcast_to(mine[None], part.shape), "tensor", 0, 0)
    prod = total[:, :R].transpose(1, 0, 2).reshape(R, n * 128)
    if not with_gram:
        return prod, None
    return prod, total[:, R : R + R // n, :R].reshape(R, R)


def inverse_factor_kernel(gram_ref, out_ref):
    shape = (8, 2 * R)
    lanes = lax.broadcasted_iota(jnp.int32, shape, 1)
    sub = lax.broadcasted_iota(jnp.int32, shape, 0)
    n = R // 8
    tiles = []
    for i in range(n):
        tile = jnp.concatenate(
            [gram_ref[8 * i : 8 * i + 8, :], jnp.zeros((8, R), jnp.float32)], axis=1
        )
        tiles.append(jnp.where(lanes == sub + (R + 8 * i), 1.0, tile))

    def column(x, j):
        return jnp.broadcast_to(x[:, j : j + 1], shape)

    def row(x, j):
        return jnp.broadcast_to(x[j : j + 1, :], shape)

    for t in range(n):
        block = tiles[t]
        cols = [column(block, 8 * t + k) for k in range(8)]
        below = [[column(tiles[i], 8 * t + k) for k in range(8)] for i in range(t + 1, n)]
        out = block
        for s in range(8):
            here = sub == s
            pivot = row(cols[s], s)
            inv = 1.0 / pivot
            factor = cols[s] * inv
            for k in range(s + 1, 8):
                across = row(cols[k], s)
                cols[k] = jnp.where(here, across * inv, cols[k] - factor * across)
            across = row(block, s)
            out = jnp.where(here, across * lax.rsqrt(pivot), out)
            block = jnp.where(here, across * inv, block - factor * across)
        out_ref[8 * t : 8 * t + 8, :] = out[:, R:]
        rows = [row(block, k) for k in range(8)]
        for i in range(t + 1, n):
            terms = [c * r for c, r in zip(below[i - t - 1], rows)]
            while len(terms) > 1:
                terms = [terms[k] + terms[k + 1] for k in range(0, len(terms), 2)]
            tiles[i] = tiles[i] - terms[0]


def inverse_factor(gram):
    return pl.pallas_call(
        inverse_factor_kernel,
        out_shape=jax.ShapeDtypeStruct((R, R), jnp.float32),
        compiler_params=pltpu.CompilerParams(vmem_limit_bytes=4 * 1024 * 1024),
        cost_estimate=pl.CostEstimate(flops=10_000_000, bytes_accessed=32768, transcendentals=128),
    )(gram)


def apply_left(factor, m):
    return jnp.dot(factor, m, precision=HIGH, preferred_element_type=jnp.float32)


def partner(flip):
    return [(i, i ^ flip) for i in range(lax.axis_size("dp"))]


def along_ring(step):
    sources = [(z + step if z % 2 == 0 else z - step) % NZ for z in range(NZ)]
    return [(2 * sources[z] + c, 2 * z + c) for z in range(NZ) for c in range(2)]


def feature_totals(part, firsts, gram, range_t=None):
    n = part.shape[1]
    first_core, first_part = firsts[n // 2]
    left, right = part[:, : n // 2], part[:, n // 2 :]
    kept = jnp.where(first_core, left, right)
    sent = jnp.where(first_core, right, left)
    half = kept + lax.ppermute(sent, "dp", partner(1))
    factor = None if gram is None else inverse_factor(gram)
    if n <= 512:
        half = half + lax.ppermute(half, "dp", partner(2))
        near, next_near, far = [lax.ppermute(half, "dp", along_ring(k)) for k in (-1, 2, -3)]
        half = (half + far) + (near + next_near)
    else:
        upper, lower = half[: R // 2], half[R // 2 :]
        kept = jnp.where(first_part, upper, lower)
        sent = jnp.where(first_part, lower, upper)
        mine = kept + lax.ppermute(sent, "dp", partner(2))
        near, across, far = [lax.ppermute(mine, "dp", partner(2 * k)) for k in (2, 7, 5)]
        mine = (mine + near) + (far + across)
        if factor is not None:
            mine, factor = lax.optimization_barrier((mine, factor))
        other = lax.ppermute(mine, "dp", partner(2))
        half = jnp.concatenate(
            [jnp.where(first_part, mine, other), jnp.where(first_part, other, mine)], axis=0
        )
    if factor is not None:
        half, factor = lax.optimization_barrier((half, factor))
        half = apply_left(factor, half)
    other = lax.ppermute(half, "dp", partner(1))
    full = jnp.concatenate(
        [jnp.where(first_core, half, other), jnp.where(first_core, other, half)], axis=1
    )
    return full if range_t is None else (full, apply_left(factor, range_t))


def per_device(acts, grads, sketch, picks):
    token_count_overall = picks.shape[0] * lax.axis_size("dp")
    place = place_numbers(sketch.shape[1])
    sketch, picks = lax.optimization_barrier((pieces(sketch), picks))
    widths = [acts.shape[1] // 2, grads.shape[1] // 2]
    masks = [(place[0, :n] == 0, place[1, :n] == 0) for n in widths]
    sketch, counts, masks = lax.optimization_barrier((sketch, counts_of(picks), masks))
    firsts = dict(zip(widths, masks))

    def to_features(proj, w, gram, range_t=None):
        return feature_totals(times(proj * counts, w), firsts, gram, range_t)

    proj, _ = token_totals(sketch, grads, False)
    range_t = to_features(proj, acts, None)
    for step in range(ITERS):
        proj, gram = token_totals(range_t, acts, True)
        if step == 0:
            proj, gram = apply_left(inverse_factor(gram), proj), None
        co_range = to_features(proj, grads, gram)
        proj, gram = token_totals(co_range, grads, True)
        range_t = to_features(proj, acts, gram)
    proj, gram = token_totals(range_t, acts, True)
    down, basis = to_features(proj, grads, gram, range_t)
    return (down / math.sqrt(token_count_overall), basis * math.sqrt(MODEL_WIDTH))


def solution(mesh):
    return jax.shard_map(
        per_device,
        mesh=mesh,
        in_specs=(P("dp", "tensor"), P("dp", "tensor"), P(None, "tensor"), P("dp")),
        out_specs=(P(None, "tensor"), P(None, "tensor")),
        check_vma=False,
    )
```
